32 devices in a mesh: grp: 8 (over y, x, core), dom: 4 (over z).
Axes of the slice: x: 2, y: 2, z: 4, core: 2. Of those that a mesh axis runs over, the one named last changes fastest.
Arguments:
- node_feat: bfloat16 [8192, 128], P(('grp', 'dom')), may hold values from -6 to 6
- edge_feat: bfloat16 [49152, 128], P(('grp', 'dom')), may hold values from -6 to 6
- edge_src: int32 [49152], P(('grp', 'dom')), may hold values from 0 to 287, as said below
- edge_dst: int32 [49152], P(('grp', 'dom')), may hold values from 0 to 255
- halo_send: int32 [128, 8], P(('grp', 'dom')), may hold values from 0 to 255
- halo_count: int32 [32, 4], P(('grp', 'dom')), may hold values from 0 to 8, as said below
- par_send: int32 [256, 4], P(('grp', 'dom')), may hold values from 0 to 31
- par_count: int32 [32, 8], P(('grp', 'dom')), may hold values from 1 to 4, as said below
- child_slot: int32 [8192], P(('grp', 'dom')), may hold values from 0 to 31, as said below
- pool_weight: float32 [8192], P(('grp', 'dom')), may hold values from 0.1 to 1
- parent_grad: bfloat16 [1024, 128], P(('grp', 'dom')), may hold values from -6 to 6
- edge_w1: bfloat16 [384, 128], replicated, may hold values from -0.3125 to 0.3125
- edge_b1: float32 [128], replicated, may hold values from -3 to 3
- edge_w2: bfloat16 [128, 128], replicated, may hold values from -0.5 to 0.5
- node_w1: bfloat16 [256, 128], replicated, may hold values from -0.375 to 0.375
- node_b1: float32 [128], replicated, may hold values from -3 to 3
- node_w2: bfloat16 [128, 128], replicated, may hold values from -0.5 to 0.5
Outputs:
- grad_nodes: bfloat16 [8192, 128], P(('grp', 'dom'))
- grad_edges: bfloat16 [49152, 128], P(('grp', 'dom'))
- grad_edge_w1: float32 [384, 128], replicated
- grad_edge_b1: float32 [128], replicated
- grad_edge_w2: float32 [128, 128], replicated
- grad_node_w1: float32 [256, 128], replicated
- grad_node_b1: float32 [128], replicated
- grad_node_w2: float32 [128, 128], replicated
The draws below stay inside these ranges and needn't reach their ends.
Inputs may be any that keep to these rules, and one draw needn't show every extreme that they name: `halo_count`: entry [r, j] is how many leading rows of partition r's block j of halo_send go to the partition of dom index j in r's group: 0 to itself, 1 or more to every other; in every group some partition receives 8 rows from every other one. `edge_src`: in each partition's 1536 edges the first 128 have halo sources 256 + j * 8 + s with s below the halo_count entry of the sender of dom index j for this partition; the others have own sources below 256. `par_count`: entry [r, k] is how many leading rows of partition r's block k of par_send go to the partition of grp index k with r's dom index; for every dom index some partition receives 4 rows from every grp index. `child_slot`: node n of partition (g, d) reads row k * 4 + s of parent_in, with s below par_count of partition (k, d) for grp index g.
All inputs are finite; a program needn't handle non-finite values.
Results may differ from the reference program's by a relative error of at most 0.0095.
Values may be sent and summed in bfloat16 or wider, within the bound.
A program may use at most 64 MiB of HBM per device.

```python
import math
import jax
import jax.numpy as jnp
from jax import lax

F = 128
NODE_DEV = 256
EDGE_DEV = 1536
HALO_PEER = 8
HALO_EDGE = 128
PAR_DEV = 32
PAR_PEER = 4
NODES = 8192
EDGES = 49152
PARENTS = 1024
N_GRP = 8
N_DOM = 4
DEVICES = 32


def halo_table(key):
    first = jax.random.fold_in(key, 101)
    second = jax.random.fold_in(key, 102)
    counts = jax.random.randint(first, (N_GRP, N_DOM, N_DOM), 1, HALO_PEER + 1)
    target = jax.random.randint(second, (N_GRP, 1, 1), 0, N_DOM)
    receiver = jnp.arange(N_DOM, dtype=jnp.int32)[None, None, :]
    sender = jnp.arange(N_DOM, dtype=jnp.int32)[None, :, None]
    counts = jnp.where(receiver == target, HALO_PEER, counts)
    counts = jnp.where(receiver == sender, 0, counts)
    return counts.astype(jnp.int32)


def parent_table(key):
    first = jax.random.fold_in(key, 201)
    second = jax.random.fold_in(key, 202)
    counts = jax.random.randint(first, (N_GRP, N_DOM, N_GRP), 1, PAR_PEER + 1)
    target = jax.random.randint(second, (1, N_DOM, 1), 0, N_GRP)
    receiver = jnp.arange(N_GRP, dtype=jnp.int32)[None, None, :]
    counts = jnp.where(receiver == target, PAR_PEER, counts)
    return counts.astype(jnp.int32)


def pick_slots(key, counts, block, picks):
    totals = jnp.sum(counts, -1, keepdims=True)
    chosen = jax.random.randint(key, counts.shape[:2] + (picks,), 0, totals)
    bounds = jnp.cumsum(counts, -1)
    peer = jnp.sum((chosen[..., None] >= bounds[..., None, :]).astype(jnp.int32), -1)
    starts = jnp.take_along_axis(bounds - counts, peer, -1)
    return (peer * block + chosen - starts).astype(jnp.int32)


def draw_halo_count(key, part):
    table = halo_table(key)
    return table.reshape(DEVICES, N_DOM)


def draw_edge_src(key, part):
    table = halo_table(key)
    key = jax.random.fold_in(key, 2)
    received = jnp.transpose(table, (0, 2, 1))
    halo = NODE_DEV + pick_slots(jax.random.fold_in(key, 3), received, HALO_PEER, HALO_EDGE)
    local = jax.random.randint(jax.random.fold_in(key, 4), (N_GRP, N_DOM, EDGE_DEV - HALO_EDGE), 0, NODE_DEV)
    return jnp.concatenate([halo, local.astype(jnp.int32)], -1).reshape(EDGES)


def draw_par_count(key, part):
    table = parent_table(key)
    return table.reshape(DEVICES, N_GRP)


def draw_child_slot(key, part):
    table = parent_table(key)
    key = jax.random.fold_in(key, 5)
    received = jnp.transpose(table, (2, 1, 0))
    return pick_slots(key, received, PAR_PEER, NODE_DEV).reshape(NODES)


def set_ends(array, rng, smallest, high):
    index_at = [jax.random.randint(jax.random.fold_in(rng, axis), (), 0, length) for axis, length in enumerate(array.shape)]
    longest = array.shape.index(max(array.shape))
    next_to = index_at[:longest] + [(index_at[longest] + 1) % array.shape[longest]] + index_at[longest + 1:]
    return array.at[tuple(index_at)].set(smallest).at[tuple(next_to)].set(high)


def shard_levels(rng, extent, split, smallest, top_value):
    def one(axis_at, parts):
        heights = jax.random.uniform(jax.random.fold_in(jax.random.fold_in(rng, 6), axis_at), (parts,), jnp.float32, smallest / len(split), top_value / len(split))
        return jnp.repeat(jnp.exp(heights), extent[axis_at] // parts).reshape((-1,) + (1,) * (len(extent) - axis_at - 1))

    factor_of = one(*split[0])
    for cut in split[1:]:
        factor_of = factor_of * one(*cut)
    return factor_of


def gaussian(stream_key, extent, deviation, reach, cuts=(), kind=jnp.bfloat16):
    entries = deviation * jax.random.normal(stream_key, extent, jnp.float32)
    if cuts:
        entries = entries * shard_levels(stream_key, extent, cuts, -0.22, 0.18)
    return jnp.clip(entries, -reach, reach).astype(kind)


def setup_inputs(seed: int = 0) -> dict:
    splits = jax.random.split(jax.random.key(seed), 18)
    return {
        "node_feat": gaussian(splits[0], (NODES, F), 1.0, 6.0, ((0, 32),)),
        "edge_feat": gaussian(splits[1], (EDGES, F), 1.0, 6.0, ((0, 32),)),
        "edge_src": draw_edge_src(jax.random.fold_in(splits[17], 71), 0),
        "edge_dst": set_ends(jax.random.randint(splits[3], (EDGES,), 0, NODE_DEV), jax.random.fold_in(splits[3], 1), 0, NODE_DEV - 1).astype(jnp.int32),
        "halo_send": set_ends(jax.random.randint(splits[4], (DEVICES * N_DOM, HALO_PEER), 0, NODE_DEV), jax.random.fold_in(splits[4], 1), 0, NODE_DEV - 1).astype(jnp.int32),
        "halo_count": draw_halo_count(jax.random.fold_in(splits[17], 71), 0),
        "par_send": set_ends(jax.random.randint(splits[6], (DEVICES * N_GRP, PAR_PEER), 0, PAR_DEV), jax.random.fold_in(splits[6], 1), 0, PAR_DEV - 1).astype(jnp.int32),
        "par_count": draw_par_count(jax.random.fold_in(splits[17], 71), 0),
        "child_slot": draw_child_slot(jax.random.fold_in(splits[17], 71), 0),
        "pool_weight": jnp.clip(jnp.exp(math.log(1.0) - 2.3025851 * jax.random.uniform(splits[9], (NODES,), jnp.float32) ** shard_levels(splits[9], (NODES,), ((0, 32),), -0.2, 0.2)), 0.1, 1.0),
        "parent_grad": gaussian(splits[10], (PARENTS, F), 1.0, 6.0, ((0, 32),)),
        "edge_w1": gaussian(splits[11], (3 * F, F), (3 * F) ** -0.5, 0.3125),
        "edge_b1": gaussian(splits[12], (F,), 0.5, 3.0, (), jnp.float32),
        "edge_w2": gaussian(splits[13], (F, F), F ** -0.5, 0.5),
        "node_w1": gaussian(splits[14], (2 * F, F), (2 * F) ** -0.5, 0.375),
        "node_b1": gaussian(splits[15], (F,), 0.5, 3.0, (), jnp.float32),
        "node_w2": gaussian(splits[16], (F, F), F ** -0.5, 0.5),
    }


def layer_norm(values):
    average = lax.optimization_barrier(jnp.mean(values, -1, keepdims=True))
    centred = values - average
    inverse = lax.rsqrt(lax.optimization_barrier(jnp.mean(centred * centred, -1, keepdims=True)) + 1e-05)
    return (centred * inverse, inverse)

def norm_back(grad, normed, inverse):
    first = lax.optimization_barrier(jnp.mean(grad, -1, keepdims=True))
    second = lax.optimization_barrier(jnp.mean(grad * normed, -1, keepdims=True))
    return inverse * (grad - first - normed * second)

def silu_slope(values):
    sigmoid = jax.nn.sigmoid(values)
    return sigmoid * (1.0 + values * (1.0 - sigmoid))

def left_product(left, right):
    return lax.dot_general(left, right, (((0,), (0,)), ((), ())), preferred_element_type=jnp.float32)

def reference(node_feat, edge_feat, edge_src, edge_dst, halo_send, halo_count, par_send, par_count, child_slot, pool_weight, parent_grad, edge_w1, edge_b1, edge_w2, node_w1, node_b1, node_w2):
    halo_rows = N_DOM * HALO_PEER
    node_base = (jnp.arange(DEVICES, dtype=jnp.int32) * NODE_DEV)[:, None, None]
    halo_index = node_base + halo_send.reshape(DEVICES, N_DOM, HALO_PEER)
    halo_valid = jnp.arange(HALO_PEER, dtype=jnp.int32)[None, None, :] < halo_count[:, :, None]
    sent = jnp.where(halo_valid[..., None], node_feat[halo_index], jnp.zeros((), node_feat.dtype))
    incoming = jnp.transpose(sent.reshape(N_GRP, N_DOM, N_DOM, HALO_PEER, F), (0, 2, 1, 3, 4)).reshape(DEVICES, halo_rows, F)
    parent_base = (jnp.arange(DEVICES, dtype=jnp.int32) * PAR_DEV)[:, None, None]
    parent_index = parent_base + par_send.reshape(DEVICES, N_GRP, PAR_PEER)
    parent_valid = jnp.arange(PAR_PEER, dtype=jnp.int32)[None, None, :] < par_count[:, :, None]
    parent_out = jnp.where(parent_valid[..., None], parent_grad[parent_index], jnp.zeros((), parent_grad.dtype))
    parent_in = jnp.transpose(parent_out.reshape(N_GRP, N_DOM, N_GRP, PAR_PEER, F), (2, 1, 0, 3, 4)).reshape(DEVICES, N_GRP * PAR_PEER, F)

    def partition(carry, pieces):
        nodes, edges, source, target, halo, parents, slots, weights = pieces
        extended = jnp.concatenate([nodes, halo], 0)
        edge_in = jnp.concatenate([edges, extended[source], extended[target]], 1)
        edge_pre = jnp.dot(edge_in, edge_w1, preferred_element_type=jnp.float32) + edge_b1
        edge_act = jax.nn.silu(edge_pre).astype(jnp.bfloat16)
        edge_hat, edge_inv = layer_norm(jnp.dot(edge_act, edge_w2, preferred_element_type=jnp.float32))
        edge_new = edges.astype(jnp.float32) + edge_hat
        gathered = jax.ops.segment_sum(edge_new, target, NODE_DEV).astype(jnp.bfloat16)
        node_in = jnp.concatenate([nodes, gathered], 1)
        node_pre = jnp.dot(node_in, node_w1, preferred_element_type=jnp.float32) + node_b1
        node_act = jax.nn.silu(node_pre).astype(jnp.bfloat16)
        node_hat, node_inv = layer_norm(jnp.dot(node_act, node_w2, preferred_element_type=jnp.float32))
        grad_out = weights[:, None] * parents[slots].astype(jnp.float32)
        grad_lin = norm_back(grad_out, node_hat, node_inv).astype(jnp.bfloat16)
        grad_nw2 = left_product(node_act, grad_lin)
        grad_act = jnp.dot(grad_lin, node_w2.T, preferred_element_type=jnp.float32)
        grad_pre = (grad_act * silu_slope(node_pre)).astype(jnp.bfloat16)
        grad_nw1 = left_product(node_in, grad_pre)
        grad_nb1 = lax.optimization_barrier(jnp.sum(grad_pre.astype(jnp.float32), 0))
        grad_node_in = jnp.dot(grad_pre, node_w1.T, preferred_element_type=jnp.float32)
        grad_new = grad_node_in[:, F:][target]
        grad_elin = norm_back(grad_new, edge_hat, edge_inv).astype(jnp.bfloat16)
        grad_ew2 = left_product(edge_act, grad_elin)
        grad_eact = jnp.dot(grad_elin, edge_w2.T, preferred_element_type=jnp.float32)
        grad_epre = (grad_eact * silu_slope(edge_pre)).astype(jnp.bfloat16)
        grad_ew1 = left_product(edge_in, grad_epre)
        grad_eb1 = lax.optimization_barrier(jnp.sum(grad_epre.astype(jnp.float32), 0))
        grad_ein = jnp.dot(grad_epre, edge_w1.T, preferred_element_type=jnp.float32)
        grad_edges = (grad_new + grad_ein[:, :F]).astype(jnp.bfloat16)
        grad_ext = jax.ops.segment_sum(grad_ein[:, F:2 * F], source, NODE_DEV + halo_rows)
        grad_ext = grad_ext + jax.ops.segment_sum(grad_ein[:, 2 * F:], target, NODE_DEV + halo_rows)
        own = grad_out + grad_node_in[:, :F] + grad_ext[:NODE_DEV]
        terms = (grad_ew1, grad_eb1, grad_ew2, grad_nw1, grad_nb1, grad_nw2)
        carry = tuple((total + term for total, term in zip(carry, terms)))
        return (carry, (own, grad_ext[NODE_DEV:], grad_edges))
    start = (jnp.zeros((3 * F, F), jnp.float32), jnp.zeros((F,), jnp.float32), jnp.zeros((F, F), jnp.float32), jnp.zeros((2 * F, F), jnp.float32), jnp.zeros((F,), jnp.float32), jnp.zeros((F, F), jnp.float32))
    inputs = (node_feat.reshape(DEVICES, NODE_DEV, F), edge_feat.reshape(DEVICES, EDGE_DEV, F), edge_src.reshape(DEVICES, EDGE_DEV), edge_dst.reshape(DEVICES, EDGE_DEV), incoming, parent_in, child_slot.reshape(DEVICES, NODE_DEV), pool_weight.reshape(DEVICES, NODE_DEV))
    totals, (own, halo_back, grad_edges) = lax.scan(partition, start, inputs)
    back = jnp.transpose(halo_back.reshape(N_GRP, N_DOM, N_DOM, HALO_PEER, F), (0, 2, 1, 3, 4)).reshape(DEVICES, N_DOM, HALO_PEER, F)
    back = jnp.where(halo_valid[..., None], back, jnp.zeros((), back.dtype))
    grad_nodes = own.reshape(NODES, F).at[halo_index.reshape(-1)].add(back.reshape(-1, F))
    scaled = tuple((total / DEVICES for total in totals))
    return (grad_nodes.astype(jnp.bfloat16), grad_edges.reshape(EDGES, F), scaled[0], scaled[1], scaled[2], scaled[3], scaled[4], scaled[5])
```

```python
import functools

import jax
import jax.numpy as jnp
from jax import lax
from jax.experimental import pallas as pl
from jax.experimental.pallas import tpu as pltpu
from jax.sharding import PartitionSpec as P

F32, BF16 = jnp.float32, jnp.bfloat16
HALO_EDGES = 128
CHUNK = 352
SLOT = 8


def round_up(value, step):
    return -(-value // step) * step


def dot(left, right):
    return jnp.dot(left, right, preferred_element_type=F32)


def dot_nt(left, right):
    return lax.dot_general(left, right, (((1,), (1,)), ((), ())), preferred_element_type=F32)


def dot_tn(left, right):
    return lax.dot_general(left, right, (((0,), (0,)), ((), ())), preferred_element_type=F32)


def sigmoid(values):
    return 0.5 * jnp.tanh(0.5 * values) + 0.5


def mean(values):
    return jnp.mean(values, -1, keepdims=True)


def layer_norm(values):
    centred = values - mean(values)
    inverse = lax.rsqrt(mean(centred * centred) + 1e-05)
    return centred * inverse, inverse


def spread(row):
    return jnp.concatenate(
        [
            jnp.transpose(jnp.broadcast_to(row[:, at : at + 128], (128, 128)))
            for at in range(0, row.shape[1], 128)
        ],
        0,
    )


def hot_columns(spread_index, columns):
    parts = []
    for at in range(0, columns, 128):
        wide = min(128, columns - at)
        lanes = at + lax.broadcasted_iota(jnp.int32, (spread_index.shape[0], wide), 1)
        parts.append((spread_index[:, :wide] == lanes).astype(F32).astype(BF16))
    return parts[0] if len(parts) == 1 else jnp.concatenate(parts, 1)


def hot_rows(row, rows):
    return (lax.broadcasted_iota(jnp.int32, (rows, row.shape[1]), 0) == row).astype(F32).astype(BF16)


def masked_index(send, count, stride):
    peers, slots = send.shape
    parts = []
    for peer in range(peers):
        valid = lax.broadcasted_iota(jnp.int32, (1, slots), 1) < count[:, peer : peer + 1]
        parts.append(jnp.where(valid, send[peer : peer + 1, :], -1))
        if stride > slots:
            parts.append(jnp.full((1, stride - slots), -1, jnp.int32))
    return jnp.concatenate(parts, 1)


def kernel(
    groups, domains,
    node_ref, edge_ref, src_ref, dst_ref, hsend_ref, hcount_ref, psend_ref, pcount_ref,
    child_ref, pool_ref, parent_ref, ew1_ref, eb1_ref, ew2_ref, nw1_ref, nb1_ref, nw2_ref,
    gnodes_ref, gedges_ref, gew1_ref, geb1_ref, gew2_ref, gnw1_ref, gnb1_ref, gnw2_ref,
    src_cols, dst_cols, src_rows, dst_rows, dst_hot, slope, inverse, act, hat, elin, epre,
    halo_out, halo_in, par_out, par_in, ret_out, ret_in,
    a_out, a_in, a_mid, a_all, b_out, b_in, b_mid, b_all,
    g_send, g_recv, d_send, d_recv,
):
    width = 128
    own, edges = node_ref.shape[0], edge_ref.shape[0]
    halo = domains * SLOT
    par_slots = psend_ref.shape[1]
    me_g, me_d = lax.axis_index("grp"), lax.axis_index("dom")

    barrier = pltpu.get_barrier_semaphore()
    for step in range(1, groups):
        pl.semaphore_signal(
            barrier, inc=1, device_id={"grp": lax.rem(me_g + step, groups)},
            device_id_type=pl.DeviceIdType.MESH,
        )
    for step in range(1, domains):
        pl.semaphore_signal(
            barrier, inc=1, device_id={"dom": lax.rem(me_d + step, domains)},
            device_id_type=pl.DeviceIdType.MESH,
        )

    def exchange(axis, phase, source, target):
        size, me = (groups, me_g) if axis == "grp" else (domains, me_d)
        send, recv = (g_send, g_recv) if axis == "grp" else (d_send, d_recv)
        copies = []
        for step in range(1, size):
            peer = lax.rem(me + step, size)
            copy = pltpu.make_async_remote_copy(
                src_ref=source(peer), dst_ref=target,
                send_sem=send.at[phase, step], recv_sem=recv.at[phase, step],
                device_id={axis: peer}, device_id_type=pl.DeviceIdType.MESH,
            )
            copy.start()
            copies.append(copy)
        return copies

    def arrive(copies):
        for copy in copies:
            copy.wait_recv()

    nodes = node_ref[...]
    halo_index = masked_index(hsend_ref[...], hcount_ref[...], SLOT)
    halo_hot = hot_rows(halo_index, own)
    sent = dot_tn(halo_hot, nodes)
    par_index = masked_index(psend_ref[...], pcount_ref[...], SLOT)
    par_sent = dot_tn(hot_rows(par_index, parent_ref.shape[0]), parent_ref[...])
    for peer in range(domains):
        halo_out[peer] = sent[peer * SLOT : (peer + 1) * SLOT]
    for peer in range(groups):
        par_out[peer] = par_sent[peer * SLOT : (peer + 1) * SLOT]
    halo_in[me_d] = halo_out[me_d]
    par_in[me_g] = par_out[me_g]
    pl.semaphore_wait(barrier, groups + domains - 2)
    halo_copies = exchange("dom", 0, lambda peer: halo_out.at[peer], halo_in.at[me_d])
    par_copies = exchange("grp", 0, lambda peer: par_out.at[peer], par_in.at[me_g])

    @pl.loop(0, edges // 128)
    def _(step):
        at = pl.ds(pl.multiple_of(step * 128, 128), 128)
        src, dst = src_ref[:, at], dst_ref[:, at]
        src_cols[at, :] = spread(src)
        dst_cols[at, :] = spread(dst)
        src_rows[:, at] = hot_rows(src, own)
        dst_rows[:, at] = hot_rows(dst, own)

    src_term = dot(nodes, ew1_ref[width : 2 * width]).astype(BF16)
    dst_term = dot(nodes, ew1_ref[2 * width :]).astype(BF16)
    eb1 = eb1_ref[...]

    def forward(at, src_part):
        hot = hot_columns(dst_cols[at, :], own)
        dst_hot[at, :] = hot
        pre = dot(edge_ref[at, :], ew1_ref[:width]) + dot(hot, dst_term) + src_part + eb1
        gate = sigmoid(pre)
        active = pre * gate
        slope[at, :] = gate + active * (1.0 - gate)
        active = active.astype(BF16)
        act[at, :] = active
        normed, inv = layer_norm(dot(active, ew2_ref[...]))
        hat[at, :] = normed.astype(BF16)
        inverse[at, :] = jnp.broadcast_to(inv, normed.shape)

    @pl.loop(0, (edges - HALO_EDGES) // CHUNK)
    def _(step):
        at = pl.ds(pl.multiple_of(HALO_EDGES + step * CHUNK, 32), CHUNK)
        forward(at, dot(hot_columns(src_cols[at, :], own), src_term))

    feature_sum = dot(dst_rows[...], edge_ref[...])
    pool = spread(pool_ref[...])
    child = child_ref[...]
    child = (child // par_slots) * SLOT + lax.rem(child, par_slots)
    child_hot = hot_columns(spread(child), groups * SLOT)

    first = pl.ds(0, HALO_EDGES)
    arrive(halo_copies)
    halo_rows = halo_in[...].reshape(halo, width).astype(BF16)
    halo_term = dot(halo_rows, ew1_ref[width : 2 * width]).astype(BF16)
    forward(first, dot(hot_columns(src_cols[first, :] - own, halo), halo_term))

    agg = (feature_sum + dot(dst_rows[...], hat[...])).astype(BF16)
    node_pre = dot(nodes, nw1_ref[:width]) + dot(agg, nw1_ref[width:]) + nb1_ref[...]
    gate = sigmoid(node_pre)
    node_act = node_pre * gate
    node_slope = gate + node_act * (1.0 - gate)
    node_act = node_act.astype(BF16)
    node_hat, node_inv = layer_norm(dot(node_act, nw2_ref[...]))
    arrive(par_copies)
    parents = par_in[...].reshape(groups * SLOT, width).astype(BF16)
    grad_out = pool * dot(child_hot, parents)
    grad_lin = (
        node_inv * (grad_out - mean(grad_out) - node_hat * mean(grad_out * node_hat))
    ).astype(BF16)
    grad_pre = dot_nt(grad_lin, nw2_ref[...]) * node_slope
    grad_pre = grad_pre.astype(BF16)
    grad_agg = dot_nt(grad_pre, nw1_ref[width:])
    agg_terms = jnp.concatenate([grad_agg, grad_agg - mean(grad_agg)], 1).astype(BF16)

    def backward(at):
        both = dot(dst_hot[at, :], agg_terms)
        grad_new, centred = both[:, :width], both[:, width:]
        normed = hat[at, :].astype(F32)
        lin = (inverse[at, :] * (centred - normed * mean(grad_new * normed))).astype(BF16)
        elin[at, :] = lin
        pre = (dot_nt(lin, ew2_ref[...]) * slope[at, :]).astype(BF16)
        epre[at, :] = pre
        gedges_ref[at, :] = (grad_new + dot_nt(pre, ew1_ref[:width])).astype(BF16)

    backward(first)
    halo_hot_rows = hot_rows(src_ref[:, :HALO_EDGES] - own, halo)
    halo_sum = dot(halo_hot_rows, epre[first, :]).astype(BF16)
    halo_grad = dot_nt(halo_sum, ew1_ref[width : 2 * width])
    for peer in range(domains):
        ret_out[peer] = halo_grad[peer * SLOT : (peer + 1) * SLOT]
    ret_in[me_d] = ret_out[me_d]
    ret_copies = exchange("dom", 1, lambda peer: ret_out.at[peer], ret_in.at[me_d])

    def bias_block(ref, at, row):
        rows = ref.shape[0] - at
        top = lax.broadcasted_iota(jnp.int32, (rows, width), 0) == 0
        ref[at:, :] = jnp.where(top, row, 0.0).astype(BF16)

    def scatter_start(phase, out, block, landing):
        landing[me_g] = out[pl.ds(pl.multiple_of(me_g * block, 16), block), :]
        return exchange(
            "grp", phase,
            lambda peer: out.at[pl.ds(pl.multiple_of(peer * block, 16), block)],
            landing.at[me_g],
        )

    def total(ref):
        value = ref[0].astype(F32)
        for at in range(1, ref.shape[0]):
            value = value + ref[at].astype(F32)
        return value

    def middle_start(phase, landing, mid):
        mid[me_d] = total(landing).astype(BF16)
        return exchange("dom", phase, lambda peer: mid.at[me_d], mid.at[me_d])

    def gather_start(phase, mid, block, everything):
        mine = pl.ds(pl.multiple_of(me_g * block, 16), block)
        everything[mine, :] = (total(mid) * (1.0 / (groups * domains))).astype(BF16)
        return exchange("grp", phase, lambda peer: everything.at[mine], everything.at[mine])

    a_block, b_block = a_in.shape[1], b_in.shape[1]
    a_out[:width, :] = dot_tn(nodes, grad_pre).astype(BF16)
    a_out[width : 2 * width, :] = dot_tn(agg, grad_pre).astype(BF16)
    a_out[2 * width : 3 * width, :] = dot_tn(node_act, grad_lin).astype(BF16)
    bias_block(a_out, 3 * width, jnp.sum(grad_pre.astype(F32), 0, keepdims=True))
    a1 = scatter_start(1, a_out, a_block, a_in)

    @pl.loop(0, (edges - HALO_EDGES) // CHUNK)
    def _(step):
        backward(pl.ds(pl.multiple_of(HALO_EDGES + step * CHUNK, 32), CHUNK))

    arrive(a1)
    a2 = middle_start(2, a_in, a_mid)

    src_sum = dot(src_rows[...], epre[...])
    dst_sum = dot(dst_rows[...], epre[...])
    src_half, dst_half = src_sum.astype(BF16), dst_sum.astype(BF16)
    b_out[:width, :] = dot_tn(edge_ref[...], epre[...]).astype(BF16)
    b_out[width : 2 * width, :] = (
        dot_tn(nodes, src_half) + dot_tn(halo_rows, halo_sum)
    ).astype(BF16)
    b_out[2 * width : 3 * width, :] = dot_tn(nodes, dst_half).astype(BF16)
    b_out[3 * width : 4 * width, :] = dot_tn(act[...], elin[...]).astype(BF16)
    bias_block(b_out, 4 * width, jnp.sum(dst_sum, 0, keepdims=True))
    b1 = scatter_start(2, b_out, b_block, b_in)

    arrive(a2)
    a3 = gather_start(3, a_mid, a_block, a_all)

    grad_self = dot_nt(grad_pre, nw1_ref[:width])
    grad_ext = dot_nt(src_half, ew1_ref[width : 2 * width]) + dot_nt(dst_half, ew1_ref[2 * width :])
    arrive(ret_copies)
    returned = dot(halo_hot, ret_in[...].reshape(halo, width).astype(BF16))
    gnodes_ref[...] = (grad_out + grad_self + grad_ext + returned).astype(BF16)

    arrive(b1)
    b2 = middle_start(3, b_in, b_mid)
    arrive(a3)
    gnw1_ref[...] = a_all[: 2 * width, :].astype(F32)
    gnw2_ref[...] = a_all[2 * width : 3 * width, :].astype(F32)
    gnb1_ref[...] = a_all[3 * width : 3 * width + 16, :].astype(F32)[:1]
    arrive(b2)
    b3 = gather_start(4, b_mid, b_block, b_all)
    arrive(b3)
    gew1_ref[...] = b_all[: 3 * width, :].astype(F32)
    gew2_ref[...] = b_all[3 * width : 4 * width, :].astype(F32)
    geb1_ref[...] = b_all[4 * width : 4 * width + 16, :].astype(F32)[:1]
    for copies in (halo_copies, par_copies, ret_copies, a1, a2, a3, b1, b2, b3):
        for copy in copies:
            copy.wait_send()


def local(groups, domains, *args):
    (
        node_feat, edge_feat, edge_src, edge_dst, halo_send, halo_count, par_send, par_count,
        child_slot, pool_weight, parent_grad, edge_w1, edge_b1, edge_w2, node_w1, node_b1, node_w2,
    ) = args
    own, width = node_feat.shape
    edges = edge_feat.shape[0]
    a_block = round_up(-(-(3 * width + 16) // groups), 16)
    b_block = round_up(-(-(4 * width + 16) // groups), 16)
    vmem = pltpu.VMEM
    scratch = [
        vmem((edges, width), jnp.int32),
        vmem((edges, width), jnp.int32),
        vmem((own, edges), BF16),
        vmem((own, edges), BF16),
        vmem((edges, own), BF16),
        vmem((edges, width), F32),
        vmem((edges, width), F32),
        vmem((edges, width), BF16),
        vmem((edges, width), BF16),
        vmem((edges, width), BF16),
        vmem((edges, width), BF16),
        vmem((domains, SLOT, width), F32),
        vmem((domains, SLOT, width), F32),
        vmem((groups, SLOT, width), F32),
        vmem((groups, SLOT, width), F32),
        vmem((domains, SLOT, width), F32),
        vmem((domains, SLOT, width), F32),
    ]
    for block in (a_block, b_block):
        scratch += [
            vmem((groups * block, width), BF16),
            vmem((groups, block, width), BF16),
            vmem((domains, block, width), BF16),
            vmem((groups * block, width), BF16),
        ]
    scratch += [
        pltpu.SemaphoreType.DMA((5, groups)),
        pltpu.SemaphoreType.DMA((5, groups)),
        pltpu.SemaphoreType.DMA((4, domains)),
        pltpu.SemaphoreType.DMA((4, domains)),
    ]
    shape = jax.ShapeDtypeStruct
    outs = pl.pallas_call(
        functools.partial(kernel, groups, domains),
        out_shape=(
            shape((own, width), BF16),
            shape((edges, width), BF16),
            shape((3 * width, width), F32),
            shape((1, width), F32),
            shape((width, width), F32),
            shape((2 * width, width), F32),
            shape((1, width), F32),
            shape((width, width), F32),
        ),
        in_specs=[pl.BlockSpec(memory_space=vmem)] * 17,
        out_specs=(pl.BlockSpec(memory_space=vmem),) * 8,
        scratch_shapes=scratch,
        compiler_params=pltpu.CompilerParams(
            collective_id=0, has_side_effects=True, vmem_limit_bytes=40 * 1024 * 1024
        ),
        name="message_layer_grad",
    )(
        node_feat, edge_feat, edge_src[None, :], edge_dst[None, :], halo_send, halo_count,
        par_send, par_count, child_slot[None, :], pool_weight[None, :], parent_grad,
        edge_w1, edge_b1[None, :], edge_w2, node_w1, node_b1[None, :], node_w2,
    )
    return (
        outs[0], outs[1], outs[2], outs[3].reshape(width), outs[4],
        outs[5], outs[6].reshape(width), outs[7],
    )


def solution(mesh):
    rows, flat = P(("grp", "dom"), None), P(("grp", "dom"))
    in_specs = (
        rows, rows, flat, flat, rows, rows, rows, rows, flat, flat, rows,
        P(), P(), P(), P(), P(), P(),
    )
    out_specs = (rows, rows, P(), P(), P(), P(), P(), P())
    return jax.shard_map(
        functools.partial(local, mesh.shape["grp"], mesh.shape["dom"]),
        mesh=mesh, in_specs=in_specs, out_specs=out_specs, check_vma=False,
    )
```

```python
import functools

import jax
import jax.numpy as jnp
from jax import lax
from jax.experimental import pallas as pl
from jax.experimental.pallas import tpu as pltpu
from jax.sharding import PartitionSpec as P

F32, BF16 = jnp.float32, jnp.bfloat16
HALO_EDGES = 128
CHUNK = 704
SLOT = 8
ARGS = 17
LOAD_ORDER = (2, 3, 0, 4, 5, 6, 7, 10, 11, 1, 12, 13, 8, 9, 14, 15, 16)
FIRST_LOADS = 2


def round_up(value, step):
    return -(-value // step) * step


def dot(left, right):
    return jnp.dot(left, right, preferred_element_type=F32)


def dot_nt(left, right):
    return lax.dot_general(left, right, (((1,), (1,)), ((), ())), preferred_element_type=F32)


def dot_tn(left, right):
    return lax.dot_general(left, right, (((0,), (0,)), ((), ())), preferred_element_type=F32)


def sigmoid(values):
    return 0.5 * jnp.tanh(0.5 * values) + 0.5


def mean(values):
    return jnp.mean(values, -1, keepdims=True)


def layer_norm(values):
    centred = values - mean(values)
    inverse = lax.rsqrt(mean(centred * centred) + 1e-05)
    return centred * inverse, inverse


def spread(row):
    return jnp.concatenate(
        [
            jnp.transpose(jnp.broadcast_to(row[:, at : at + 128], (128, 128)))
            for at in range(0, row.shape[1], 128)
        ],
        0,
    )


def hot_columns(spread_index, columns):
    parts = []
    for at in range(0, columns, 128):
        wide = min(128, columns - at)
        lanes = at + lax.broadcasted_iota(jnp.int32, (spread_index.shape[0], wide), 1)
        parts.append((spread_index[:, :wide] == lanes).astype(F32).astype(BF16))
    return parts[0] if len(parts) == 1 else jnp.concatenate(parts, 1)


def hot_rows(row, rows):
    return (lax.broadcasted_iota(jnp.int32, (rows, row.shape[1]), 0) == row).astype(F32).astype(BF16)


def masked_index(send, count):
    peers, slots = send.shape
    parts = []
    for peer in range(peers):
        valid = lax.broadcasted_iota(jnp.int32, (1, slots), 1) < count[:, peer : peer + 1]
        parts.append(jnp.where(valid, send[peer : peer + 1, :], -1))
    return jnp.concatenate(parts, 1)


def kernel(
    groups, domains,
    *refs,
):
    args, outs = refs[:ARGS], refs[ARGS : ARGS + 4]
    local_refs, local_outs = refs[ARGS + 4 : 2 * ARGS + 4], refs[2 * ARGS + 4 : 2 * ARGS + 8]
    load_sem, store_sem = refs[2 * ARGS + 8 : 2 * ARGS + 10]
    loads = []
    for at in LOAD_ORDER:
        load = pltpu.make_async_copy(args[at], local_refs[at], load_sem.at[at])
        load.start()
        loads.append(load)
    stores = [
        pltpu.make_async_copy(local_outs[at], outs[at], store_sem.at[at]) for at in range(4)
    ]
    body(groups, domains, loads, stores, *local_refs, *local_outs, *refs[2 * ARGS + 10 :])


def body(
    groups, domains, loads, stores,
    node_ref, edge_ref, src_ref, dst_ref, hsend_ref, hcount_ref, psend_ref, pcount_ref,
    child_ref, pool_ref, parent_ref, ew1_ref, eb1_ref, ew2_ref, nw1_ref, nb1_ref, nw2_ref,
    gnodes_ref, gedges_ref, a_all, b_all,
    src_cols, dst_cols, src_rows, dst_rows, dst_hot, slope, inverse, act, hat, elin, epre,
    halo_out, halo_in, par_out, par_in, ret_out, ret_in,
    a_out, a_in, a_mid, b_out, b_in, b_mid,
    g_send, g_recv, d_send, d_recv,
):
    width = 128
    own, edges = node_ref.shape[0], edge_ref.shape[0]
    halo = domains * SLOT
    par_slots = psend_ref.shape[0]
    me_g, me_d = lax.axis_index("grp"), lax.axis_index("dom")

    barrier = pltpu.get_barrier_semaphore()
    for step in range(1, groups):
        pl.semaphore_signal(
            barrier, inc=1, device_id={"grp": lax.rem(me_g + step, groups)},
            device_id_type=pl.DeviceIdType.MESH,
        )
    for step in range(1, domains):
        pl.semaphore_signal(
            barrier, inc=1, device_id={"dom": lax.rem(me_d + step, domains)},
            device_id_type=pl.DeviceIdType.MESH,
        )

    def exchange(axis, phase, source, target):
        size, me = (groups, me_g) if axis == "grp" else (domains, me_d)
        send, recv = (g_send, g_recv) if axis == "grp" else (d_send, d_recv)
        copies = []
        for step in range(1, size):
            peer = lax.rem(me + step, size)
            copy = pltpu.make_async_remote_copy(
                src_ref=source(peer), dst_ref=target,
                send_sem=send.at[phase, step], recv_sem=recv.at[phase, step],
                device_id={axis: peer}, device_id_type=pl.DeviceIdType.MESH,
            )
            copy.start()
            copies.append(copy)
        return copies

    def arrive(copies):
        for copy in copies:
            copy.wait_recv()

    for load in loads[:FIRST_LOADS]:
        load.wait()

    @pl.loop(0, edges // 128, unroll=4)
    def _(step):
        at = pl.ds(pl.multiple_of(step * 128, 128), 128)
        src, dst = src_ref[pl.ds(step, 1), :], dst_ref[pl.ds(step, 1), :]
        src_cols[at, :] = spread(src)
        dst_cols[at, :] = spread(dst)
        src_rows[:, at] = hot_rows(src, own)
        dst_rows[:, at] = hot_rows(dst, own)

    for load in loads[FIRST_LOADS:]:
        load.wait()
    nodes = node_ref[...]
    halo_index = masked_index(hsend_ref[...], hcount_ref[...])
    halo_hot = hot_rows(halo_index, own)
    sent = dot_tn(halo_hot, nodes)
    par_index = jnp.concatenate(
        [
            jnp.where(at < pcount_ref[...], psend_ref[at : at + 1, :], -1)
            for at in range(par_slots)
        ],
        1,
    )
    par_sent = dot_tn(hot_rows(par_index, parent_ref.shape[0]), parent_ref[...])
    for peer in range(domains):
        halo_out[peer] = sent[peer * SLOT : (peer + 1) * SLOT]
    par_out[...] = jnp.zeros_like(par_out)
    for at in range(par_slots):
        par_out[:, at, :] = par_sent[at * groups : (at + 1) * groups]
    halo_in[me_d] = halo_out[me_d]
    par_in[me_g] = par_out[me_g]
    pl.semaphore_wait(barrier, groups + domains - 2)
    halo_copies = exchange("dom", 0, lambda peer: halo_out.at[peer], halo_in.at[me_d])
    par_copies = exchange("grp", 0, lambda peer: par_out.at[peer], par_in.at[me_g])

    src_term = dot(nodes, ew1_ref[width : 2 * width]).astype(BF16)
    dst_term = dot(nodes, ew1_ref[2 * width :]).astype(BF16)
    eb1 = eb1_ref[...]

    def forward(at, src_part):
        hot = hot_columns(dst_cols[at, :], own)
        dst_hot[at, :] = hot
        pre = dot(edge_ref[at, :], ew1_ref[:width]) + dot(hot, dst_term) + src_part + eb1
        gate = sigmoid(pre)
        active = pre * gate
        slope[at, :] = gate + active * (1.0 - gate)
        active = active.astype(BF16)
        act[at, :] = active
        normed, inv = layer_norm(dot(active, ew2_ref[...]))
        hat[at, :] = normed.astype(BF16)
        inverse[at, :] = jnp.broadcast_to(inv, normed.shape)

    @pl.loop(0, (edges - HALO_EDGES) // CHUNK)
    def _(step):
        at = pl.ds(pl.multiple_of(HALO_EDGES + step * CHUNK, 32), CHUNK)
        forward(at, dot(hot_columns(src_cols[at, :], own), src_term))

    feature_sum = dot(dst_rows[...], edge_ref[...])
    pool = spread(pool_ref[...])
    child = child_ref[...]
    child = (child // par_slots) * SLOT + lax.rem(child, par_slots)
    child_hot = hot_columns(spread(child), groups * SLOT)

    first = pl.ds(0, HALO_EDGES)
    arrive(halo_copies)
    halo_rows = halo_in[...].reshape(halo, width).astype(BF16)
    halo_term = dot(halo_rows, ew1_ref[width : 2 * width]).astype(BF16)
    forward(first, dot(hot_columns(src_cols[first, :] - own, halo), halo_term))

    agg = (feature_sum + dot(dst_rows[...], hat[...])).astype(BF16)
    node_pre = dot(nodes, nw1_ref[:width]) + dot(agg, nw1_ref[width:]) + nb1_ref[...]
    gate = sigmoid(node_pre)
    node_act = node_pre * gate
    node_slope = gate + node_act * (1.0 - gate)
    node_act = node_act.astype(BF16)
    node_hat, node_inv = layer_norm(dot(node_act, nw2_ref[...]))
    arrive(par_copies)
    parents = par_in[...].reshape(groups * SLOT, width).astype(BF16)
    grad_out = pool * dot(child_hot, parents)
    grad_lin = (
        node_inv * (grad_out - mean(grad_out) - node_hat * mean(grad_out * node_hat))
    ).astype(BF16)
    grad_pre = dot_nt(grad_lin, nw2_ref[...]) * node_slope
    grad_pre = grad_pre.astype(BF16)
    grad_agg = dot_nt(grad_pre, nw1_ref[width:])
    agg_centred = (grad_agg - mean(grad_agg)).astype(BF16)

    def backward(at):
        centred = dot(dst_hot[at, :], agg_centred)
        normed = hat[at, :].astype(F32)
        lin = (inverse[at, :] * (centred - normed * mean(centred * normed))).astype(BF16)
        elin[at, :] = lin
        pre = (dot_nt(lin, ew2_ref[...]) * slope[at, :]).astype(BF16)
        epre[at, :] = pre

    backward(first)
    halo_hot_rows = hot_rows(jnp.concatenate([src_ref[at : at + 1, :] for at in range(HALO_EDGES // 128)], 1) - own, halo)
    halo_sum = dot(halo_hot_rows, epre[first, :]).astype(BF16)
    halo_grad = dot_nt(halo_sum, ew1_ref[width : 2 * width])
    for peer in range(domains):
        ret_out[peer] = halo_grad[peer * SLOT : (peer + 1) * SLOT]
    ret_in[me_d] = ret_out[me_d]
    ret_copies = exchange("dom", 1, lambda peer: ret_out.at[peer], ret_in.at[me_d])

    def bias_block(ref, at, row):
        rows = ref.shape[0] - at
        top = lax.broadcasted_iota(jnp.int32, (rows, width), 0) == 0
        ref[at:, :] = jnp.where(top, row, 0.0).astype(BF16)

    def scatter_start(phase, out, block, landing):
        landing[me_g] = out[pl.ds(pl.multiple_of(me_g * block, 16), block), :]
        return exchange(
            "grp", phase,
            lambda peer: out.at[pl.ds(pl.multiple_of(peer * block, 16), block)],
            landing.at[me_g],
        )

    def total(ref):
        value = ref[0].astype(F32)
        for at in range(1, ref.shape[0]):
            value = value + ref[at].astype(F32)
        return value

    def middle_start(phase, landing, mid):
        mid[me_d] = total(landing).astype(BF16)
        return exchange("dom", phase, lambda peer: mid.at[me_d], mid.at[me_d])

    def gather_start(phase, mid, block, everything):
        mine = pl.ds(pl.multiple_of(me_g * block, 16), block)
        everything[mine, :] = (total(mid) * (1.0 / (groups * domains))).astype(BF16)
        return exchange("grp", phase, lambda peer: everything.at[mine], everything.at[mine])

    a_block, b_block = a_in.shape[1], b_in.shape[1]
    a_out[:width, :] = dot_tn(nodes, grad_pre).astype(BF16)
    a_out[width : 2 * width, :] = dot_tn(agg, grad_pre).astype(BF16)
    a_out[2 * width : 3 * width, :] = dot_tn(node_act, grad_lin).astype(BF16)
    bias_block(a_out, 3 * width, jnp.sum(grad_pre.astype(F32), 0, keepdims=True))
    a1 = scatter_start(1, a_out, a_block, a_in)

    @pl.loop(0, (edges - HALO_EDGES) // CHUNK)
    def _(step):
        backward(pl.ds(pl.multiple_of(HALO_EDGES + step * CHUNK, 32), CHUNK))

    arrive(a1)
    a2 = middle_start(2, a_in, a_mid)

    src_sum = dot(src_rows[...], epre[...])
    dst_sum = dot(dst_rows[...], epre[...])
    src_half, dst_half = src_sum.astype(BF16), dst_sum.astype(BF16)
    b_out[:width, :] = dot_tn(edge_ref[...], epre[...]).astype(BF16)
    b_out[width : 2 * width, :] = (
        dot_tn(nodes, src_half) + dot_tn(halo_rows, halo_sum)
    ).astype(BF16)
    b_out[2 * width : 3 * width, :] = dot_tn(nodes, dst_half).astype(BF16)
    b_out[3 * width : 4 * width, :] = dot_tn(act[...], elin[...]).astype(BF16)
    bias_block(b_out, 4 * width, jnp.sum(dst_sum, 0, keepdims=True))
    b1 = scatter_start(2, b_out, b_block, b_in)

    grad_agg = grad_agg.astype(BF16)

    def finish(at):
        gedges_ref[at, :] = (
            dot(dst_hot[at, :], grad_agg) + dot_nt(epre[at, :], ew1_ref[:width])
        ).astype(BF16)

    finish(first)

    @pl.loop(0, (edges - HALO_EDGES) // CHUNK)
    def _(step):
        finish(pl.ds(pl.multiple_of(HALO_EDGES + step * CHUNK, 32), CHUNK))

    stores[1].start()
    arrive(a2)
    a3 = gather_start(3, a_mid, a_block, a_all)

    grad_self = dot_nt(grad_pre, nw1_ref[:width])
    grad_ext = dot_nt(src_half, ew1_ref[width : 2 * width]) + dot_nt(dst_half, ew1_ref[2 * width :])
    arrive(ret_copies)
    returned = dot(halo_hot, ret_in[...].reshape(halo, width).astype(BF16))
    gnodes_ref[...] = (grad_out + grad_self + grad_ext + returned).astype(BF16)
    stores[0].start()

    arrive(b1)
    b2 = middle_start(3, b_in, b_mid)
    arrive(a3)
    stores[2].start()
    arrive(b2)
    b3 = gather_start(4, b_mid, b_block, b_all)
    arrive(b3)
    stores[3].start()
    for copies in (halo_copies, par_copies, ret_copies, a1, a2, a3, b1, b2, b3):
        for copy in copies:
            copy.wait_send()
    for store in stores:
        store.wait()


def write_kernel(
    nodes_ref, edges_ref, a_ref, b_ref,
    gnodes_ref, gedges_ref, gew1_ref, geb1_ref, gew2_ref, gnw1_ref, gnb1_ref, gnw2_ref,
    a_local, b_local, ew1, eb1, ew2, nw1, nb1, nw2, sem,
):
    width = 128
    copies = []

    def write(source, target):
        copy = pltpu.make_async_copy(source, target, sem.at[len(copies)])
        copy.start()
        copies.append(copy)

    load_a = pltpu.make_async_copy(a_ref, a_local, sem.at[8])
    load_b = pltpu.make_async_copy(b_ref, b_local, sem.at[9])
    load_b.start()
    load_a.start()
    write(edges_ref, gedges_ref)
    write(nodes_ref, gnodes_ref)
    load_b.wait()
    load_a.wait()
    ew1[...] = b_local[: 3 * width, :].astype(F32)
    write(ew1, gew1_ref)
    nw1[...] = a_local[: 2 * width, :].astype(F32)
    write(nw1, gnw1_ref)
    ew2[...] = b_local[3 * width : 4 * width, :].astype(F32)
    write(ew2, gew2_ref)
    nw2[...] = a_local[2 * width : 3 * width, :].astype(F32)
    write(nw2, gnw2_ref)
    eb1[...] = b_local[4 * width : 4 * width + 16, :].astype(F32)[:1]
    write(eb1, geb1_ref)
    nb1[...] = a_local[3 * width : 3 * width + 16, :].astype(F32)[:1]
    write(nb1, gnb1_ref)
    for copy in copies:
        copy.wait()


def local(groups, domains, *args):
    (
        node_feat, edge_feat, edge_src, edge_dst, halo_send, halo_count, par_send, par_count,
        child_slot, pool_weight, parent_grad, edge_w1, edge_b1, edge_w2, node_w1, node_b1, node_w2,
    ) = args
    own, width = node_feat.shape
    edges = edge_feat.shape[0]
    a_block = round_up(-(-(3 * width + 16) // groups), 16)
    b_block = round_up(-(-(4 * width + 16) // groups), 16)
    vmem = pltpu.VMEM
    scratch = [
        vmem((edges, width), jnp.int32),
        vmem((edges, width), jnp.int32),
        vmem((own, edges), BF16),
        vmem((own, edges), BF16),
        vmem((edges, own), BF16),
        vmem((edges, width), F32),
        vmem((edges, width), F32),
        vmem((edges, width), BF16),
        vmem((edges, width), BF16),
        vmem((edges, width), BF16),
        vmem((edges, width), BF16),
        vmem((domains, SLOT, width), F32),
        vmem((domains, SLOT, width), F32),
        vmem((groups, SLOT, width), F32),
        vmem((groups, SLOT, width), F32),
        vmem((domains, SLOT, width), F32),
        vmem((domains, SLOT, width), F32),
    ]
    for block in (a_block, b_block):
        scratch += [
            vmem((groups * block, width), BF16),
            vmem((groups, block, width), BF16),
            vmem((domains, block, width), BF16),
        ]
    scratch += [
        pltpu.SemaphoreType.DMA((5, groups)),
        pltpu.SemaphoreType.DMA((5, groups)),
        pltpu.SemaphoreType.DMA((4, domains)),
        pltpu.SemaphoreType.DMA((4, domains)),
    ]
    shape = jax.ShapeDtypeStruct
    operands = (
        node_feat, edge_feat, edge_src.reshape(edges // 128, 128), edge_dst.reshape(edges // 128, 128),
        halo_send, halo_count, par_send.T, par_count, child_slot[None, :], pool_weight[None, :],
        parent_grad, edge_w1, edge_b1[None, :], edge_w2, node_w1, node_b1[None, :], node_w2,
    )
    results = (
        shape((own, width), BF16),
        shape((edges, width), BF16),
        shape((groups * a_block, width), BF16),
        shape((groups * b_block, width), BF16),
    )
    buffers = [vmem(array.shape, array.dtype) for array in operands + results]
    results = pl.pallas_call(
        functools.partial(kernel, groups, domains),
        out_shape=results,
        in_specs=[pl.BlockSpec(memory_space=pltpu.HBM)] * ARGS,
        out_specs=(pl.BlockSpec(memory_space=pltpu.HBM),) * 4,
        scratch_shapes=buffers
        + [pltpu.SemaphoreType.DMA((ARGS,)), pltpu.SemaphoreType.DMA((4,))]
        + scratch,
        compiler_params=pltpu.CompilerParams(
            collective_id=0, has_side_effects=True, vmem_limit_bytes=60 * 1024 * 1024
        ),
        name="message_layer_grad",
    )(*operands)
    weights = [(3 * width, width), (1, width), (width, width), (2 * width, width), (1, width), (width, width)]
    outs = pl.pallas_call(
        write_kernel,
        out_shape=(shape((own, width), BF16), shape((edges, width), BF16))
        + tuple(shape(size, F32) for size in weights),
        in_specs=[pl.BlockSpec(memory_space=pltpu.HBM)] * 4,
        out_specs=(pl.BlockSpec(memory_space=pltpu.HBM),) * 8,
        scratch_shapes=buffers[-2:]
        + [vmem(size, F32) for size in weights]
        + [pltpu.SemaphoreType.DMA((10,))],
        compiler_params=pltpu.CompilerParams(vmem_limit_bytes=60 * 1024 * 1024),
        name="write_results",
    )(*results)
    return (
        outs[0], outs[1], outs[2], outs[3].reshape(width), outs[4],
        outs[5], outs[6].reshape(width), outs[7],
    )


def solution(mesh):
    rows, flat = P(("grp", "dom"), None), P(("grp", "dom"))
    in_specs = (
        rows, rows, flat, flat, rows, rows, rows, rows, flat, flat, rows,
        P(), P(), P(), P(), P(), P(),
    )
    out_specs = (rows, rows, P(), P(), P(), P(), P(), P())
    return jax.shard_map(
        functools.partial(local, mesh.shape["grp"], mesh.shape["dom"]),
        mesh=mesh, in_specs=in_specs, out_specs=out_specs, check_vma=False,
    )
```

```python
import functools

import jax
import jax.numpy as jnp
from jax import lax
from jax.experimental import pallas as pl
from jax.experimental.pallas import tpu as pltpu
from jax.sharding import PartitionSpec as P

F32, BF16 = jnp.float32, jnp.bfloat16
HALO_EDGES = 128
CHUNK = 704
SLOT = 8
ARGS = 17
LOAD_ORDER = (2, 3, 0, 4, 5, 6, 7, 10, 11, 1, 12, 13, 8, 9, 14, 15, 16)
FIRST_LOADS = 2


def round_up(value, step):
    return -(-value // step) * step


def dot(left, right):
    return jnp.dot(left, right, preferred_element_type=F32)


def dot_nt(left, right):
    return lax.dot_general(left, right, (((1,), (1,)), ((), ())), preferred_element_type=F32)


def dot_tn(left, right):
    return lax.dot_general(left, right, (((0,), (0,)), ((), ())), preferred_element_type=F32)


def sigmoid(values):
    return 0.5 * jnp.tanh(0.5 * values) + 0.5


def mean(values):
    return jnp.mean(values, -1, keepdims=True)


def layer_norm(values):
    centred = values - mean(values)
    inverse = lax.rsqrt(mean(centred * centred) + 1e-05)
    return centred * inverse, inverse


def spread(row):
    return jnp.concatenate(
        [
            jnp.transpose(jnp.broadcast_to(row[:, at : at + 128], (128, 128)))
            for at in range(0, row.shape[1], 128)
        ],
        0,
    )


def hot_columns(spread_index, columns):
    parts = []
    for at in range(0, columns, 128):
        wide = min(128, columns - at)
        lanes = at + lax.broadcasted_iota(jnp.int32, (spread_index.shape[0], wide), 1)
        parts.append((spread_index[:, :wide] == lanes).astype(F32).astype(BF16))
    return parts[0] if len(parts) == 1 else jnp.concatenate(parts, 1)


def hot_rows(row, rows):
    return (lax.broadcasted_iota(jnp.int32, (rows, row.shape[1]), 0) == row).astype(F32).astype(BF16)


def masked_index(send, count):
    peers, slots = send.shape
    parts = []
    for peer in range(peers):
        valid = lax.broadcasted_iota(jnp.int32, (1, slots), 1) < count[:, peer : peer + 1]
        parts.append(jnp.where(valid, send[peer : peer + 1, :], -1))
    return jnp.concatenate(parts, 1)


def kernel(
    groups, domains,
    *refs,
):
    args, outs = refs[:ARGS], refs[ARGS : ARGS + 4]
    local_refs, local_outs = refs[ARGS + 4 : 2 * ARGS + 4], refs[2 * ARGS + 4 : 2 * ARGS + 8]
    load_sem, store_sem = refs[2 * ARGS + 8 : 2 * ARGS + 10]
    loads = []
    for at in LOAD_ORDER:
        load = pltpu.make_async_copy(args[at], local_refs[at], load_sem.at[at])
        load.start()
        loads.append(load)
    stores = [
        pltpu.make_async_copy(local_outs[at], outs[at], store_sem.at[at]) for at in range(4)
    ]
    body(groups, domains, loads, stores, *local_refs, *local_outs, *refs[2 * ARGS + 10 :])


def body(
    groups, domains, loads, stores,
    node_ref, edge_ref, src_ref, dst_ref, hsend_ref, hcount_ref, psend_ref, pcount_ref,
    child_ref, pool_ref, parent_ref, ew1_ref, eb1_ref, ew2_ref, nw1_ref, nb1_ref, nw2_ref,
    gnodes_ref, gedges_ref, a_all, b_all,
    src_cols, dst_cols, src_rows, dst_rows, dst_hot, slope, inverse, act, hat, elin, epre,
    halo_out, halo_in, par_out, par_in, ret_out, ret_in,
    a_out, a_in, a_mid, b_out, b_in, b_mid,
    g_send, g_recv, d_send, d_recv,
):
    width = 128
    own, edges = node_ref.shape[0], edge_ref.shape[0]
    halo = domains * SLOT
    par_slots = psend_ref.shape[0]
    me_g, me_d = lax.axis_index("grp"), lax.axis_index("dom")

    barrier = pltpu.get_barrier_semaphore()
    for step in range(1, groups):
        pl.semaphore_signal(
            barrier, inc=1, device_id={"grp": lax.rem(me_g + step, groups)},
            device_id_type=pl.DeviceIdType.MESH,
        )
    for step in range(1, domains):
        pl.semaphore_signal(
            barrier, inc=1, device_id={"dom": lax.rem(me_d + step, domains)},
            device_id_type=pl.DeviceIdType.MESH,
        )

    def exchange(axis, phase, source, target):
        size, me = (groups, me_g) if axis == "grp" else (domains, me_d)
        send, recv = (g_send, g_recv) if axis == "grp" else (d_send, d_recv)
        copies = []
        for step in range(1, size):
            peer = lax.rem(me + step, size)
            copy = pltpu.make_async_remote_copy(
                src_ref=source(peer), dst_ref=target,
                send_sem=send.at[phase, step], recv_sem=recv.at[phase, step],
                device_id={axis: peer}, device_id_type=pl.DeviceIdType.MESH,
            )
            copy.start()
            copies.append(copy)
        return copies

    def arrive(copies):
        for copy in copies:
            copy.wait_recv()

    for load in loads[:FIRST_LOADS]:
        load.wait()

    @pl.loop(0, edges // 128, unroll=4)
    def _(step):
        at = pl.ds(pl.multiple_of(step * 128, 128), 128)
        src, dst = src_ref[pl.ds(step, 1), :], dst_ref[pl.ds(step, 1), :]
        src_cols[at, :] = spread(src)
        dst_cols[at, :] = spread(dst)
        src_rows[:, at] = hot_rows(src, own)
        dst_rows[:, at] = hot_rows(dst, own)

    for load in loads[FIRST_LOADS:]:
        load.wait()
    nodes = node_ref[...]
    halo_index = masked_index(hsend_ref[...], hcount_ref[...])
    halo_hot = hot_rows(halo_index, own)
    sent = dot_tn(halo_hot, nodes)
    par_index = jnp.concatenate(
        [
            jnp.where(at < pcount_ref[...], psend_ref[at : at + 1, :], -1)
            for at in range(par_slots)
        ],
        1,
    )
    par_sent = dot_tn(hot_rows(par_index, parent_ref.shape[0]), parent_ref[...])
    for peer in range(domains):
        halo_out[peer] = sent[peer * SLOT : (peer + 1) * SLOT]
    par_out[...] = jnp.zeros_like(par_out)
    for at in range(par_slots):
        par_out[:, at, :] = par_sent[at * groups : (at + 1) * groups]
    halo_in[me_d] = halo_out[me_d]
    par_in[me_g] = par_out[me_g]
    pl.semaphore_wait(barrier, groups + domains - 2)
    halo_copies = exchange("dom", 0, lambda peer: halo_out.at[peer], halo_in.at[me_d])
    par_copies = exchange("grp", 0, lambda peer: par_out.at[peer], par_in.at[me_g])

    src_term = dot(nodes, ew1_ref[width : 2 * width]).astype(BF16)
    dst_term = dot(nodes, ew1_ref[2 * width :]).astype(BF16)
    eb1 = eb1_ref[...]

    def forward(at, src_part):
        hot = hot_columns(dst_cols[at, :], own)
        dst_hot[at, :] = hot
        pre = dot(edge_ref[at, :], ew1_ref[:width]) + dot(hot, dst_term) + src_part + eb1
        gate = sigmoid(pre)
        active = pre * gate
        slope[at, :] = gate + active * (1.0 - gate)
        active = active.astype(BF16)
        act[at, :] = active
        normed, inv = layer_norm(dot(active, ew2_ref[...]))
        hat[at, :] = normed.astype(BF16)
        inverse[at, :] = jnp.broadcast_to(inv, normed.shape)

    @pl.loop(0, (edges - HALO_EDGES) // CHUNK)
    def _(step):
        at = pl.ds(pl.multiple_of(HALO_EDGES + step * CHUNK, 32), CHUNK)
        forward(at, dot(hot_columns(src_cols[at, :], own), src_term))

    feature_sum = dot(dst_rows[...], edge_ref[...])
    pool = spread(pool_ref[...])
    child = child_ref[...]
    child = (child // par_slots) * SLOT + lax.rem(child, par_slots)
    child_hot = hot_columns(spread(child), groups * SLOT)

    first = pl.ds(0, HALO_EDGES)
    arrive(halo_copies)
    halo_rows = halo_in[...].reshape(halo, width).astype(BF16)
    halo_term = dot(halo_rows, ew1_ref[width : 2 * width]).astype(BF16)
    forward(first, dot(hot_columns(src_cols[first, :] - own, halo), halo_term))

    agg = (feature_sum + dot(dst_rows[...], hat[...])).astype(BF16)
    node_pre = dot(nodes, nw1_ref[:width]) + dot(agg, nw1_ref[width:]) + nb1_ref[...]
    gate = sigmoid(node_pre)
    node_act = node_pre * gate
    node_slope = gate + node_act * (1.0 - gate)
    node_act = node_act.astype(BF16)
    node_hat, node_inv = layer_norm(dot(node_act, nw2_ref[...]))
    arrive(par_copies)
    parents = par_in[...].reshape(groups * SLOT, width).astype(BF16)
    grad_out = pool * dot(child_hot, parents)
    grad_lin = (
        node_inv * (grad_out - mean(grad_out) - node_hat * mean(grad_out * node_hat))
    ).astype(BF16)
    grad_pre = dot_nt(grad_lin, nw2_ref[...]) * node_slope
    grad_pre = grad_pre.astype(BF16)
    grad_agg = dot_nt(grad_pre, nw1_ref[width:])
    agg_centred = (grad_agg - mean(grad_agg)).astype(BF16)

    def backward(at):
        centred = dot(dst_hot[at, :], agg_centred)
        normed = hat[at, :].astype(F32)
        lin = (inverse[at, :] * (centred - normed * mean(centred * normed))).astype(BF16)
        elin[at, :] = lin
        pre = (dot_nt(lin, ew2_ref[...]) * slope[at, :]).astype(BF16)
        epre[at, :] = pre

    backward(first)
    halo_hot_rows = hot_rows(jnp.concatenate([src_ref[at : at + 1, :] for at in range(HALO_EDGES // 128)], 1) - own, halo)
    halo_sum = dot(halo_hot_rows, epre[first, :]).astype(BF16)
    halo_grad = dot_nt(halo_sum, ew1_ref[width : 2 * width])
    for peer in range(domains):
        ret_out[peer] = halo_grad[peer * SLOT : (peer + 1) * SLOT]
    ret_in[me_d] = ret_out[me_d]
    ret_copies = exchange("dom", 1, lambda peer: ret_out.at[peer], ret_in.at[me_d])

    def bias_block(ref, at, row):
        rows = ref.shape[0] - at
        top = lax.broadcasted_iota(jnp.int32, (rows, width), 0) == 0
        ref[at:, :] = jnp.where(top, row, 0.0).astype(BF16)

    def scatter_start(phase, out, block, landing):
        landing[me_g] = out[pl.ds(pl.multiple_of(me_g * block, 16), block), :]
        return exchange(
            "grp", phase,
            lambda peer: out.at[pl.ds(pl.multiple_of(peer * block, 16), block)],
            landing.at[me_g],
        )

    def total(ref):
        value = ref[0].astype(F32)
        for at in range(1, ref.shape[0]):
            value = value + ref[at].astype(F32)
        return value

    def middle_start(phase, landing, mid):
        mid[me_d] = total(landing).astype(BF16)
        return exchange("dom", phase, lambda peer: mid.at[me_d], mid.at[me_d])

    def gather_start(phase, mid, block, everything):
        mine = pl.ds(pl.multiple_of(me_g * block, 16), block)
        everything[mine, :] = (total(mid) * (1.0 / (groups * domains))).astype(BF16)
        return exchange("grp", phase, lambda peer: everything.at[mine], everything.at[mine])

    a_block, b_block = a_in.shape[1], b_in.shape[1]
    a_out[:width, :] = dot_tn(nodes, grad_pre).astype(BF16)
    a_out[width : 2 * width, :] = dot_tn(agg, grad_pre).astype(BF16)
    a_out[2 * width : 3 * width, :] = dot_tn(node_act, grad_lin).astype(BF16)
    bias_block(a_out, 3 * width, jnp.sum(grad_pre.astype(F32), 0, keepdims=True))
    a1 = scatter_start(1, a_out, a_block, a_in)

    @pl.loop(0, (edges - HALO_EDGES) // CHUNK)
    def _(step):
        backward(pl.ds(pl.multiple_of(HALO_EDGES + step * CHUNK, 32), CHUNK))

    arrive(a1)
    a2 = middle_start(2, a_in, a_mid)

    src_sum = dot(src_rows[...], epre[...])
    dst_sum = dot(dst_rows[...], epre[...])
    src_half, dst_half = src_sum.astype(BF16), dst_sum.astype(BF16)
    b_out[:width, :] = dot_tn(edge_ref[...], epre[...]).astype(BF16)
    b_out[width : 2 * width, :] = (
        dot_tn(nodes, src_half) + dot_tn(halo_rows, halo_sum)
    ).astype(BF16)
    b_out[2 * width : 3 * width, :] = dot_tn(nodes, dst_half).astype(BF16)
    b_out[3 * width : 4 * width, :] = dot_tn(act[...], elin[...]).astype(BF16)
    bias_block(b_out, 4 * width, jnp.sum(dst_sum, 0, keepdims=True))
    b1 = scatter_start(2, b_out, b_block, b_in)

    grad_agg = grad_agg.astype(BF16)

    def finish(at):
        gedges_ref[at, :] = (
            dot(dst_hot[at, :], grad_agg) + dot_nt(epre[at, :], ew1_ref[:width])
        ).astype(BF16)

    finish(first)

    @pl.loop(0, (edges - HALO_EDGES) // CHUNK)
    def _(step):
        finish(pl.ds(pl.multiple_of(HALO_EDGES + step * CHUNK, 32), CHUNK))

    stores[1].start()
    arrive(a2)
    a3 = gather_start(3, a_mid, a_block, a_all)

    grad_self = dot_nt(grad_pre, nw1_ref[:width])
    grad_ext = dot_nt(src_half, ew1_ref[width : 2 * width]) + dot_nt(dst_half, ew1_ref[2 * width :])
    arrive(ret_copies)
    returned = dot(halo_hot, ret_in[...].reshape(halo, width).astype(BF16))
    gnodes_ref[...] = (grad_out + grad_self + grad_ext + returned).astype(BF16)
    stores[0].start()

    arrive(b1)
    b2 = middle_start(3, b_in, b_mid)
    arrive(a3)
    stores[2].start()
    arrive(b2)
    b3 = gather_start(4, b_mid, b_block, b_all)
    arrive(b3)
    stores[3].start()
    for copies in (halo_copies, par_copies, ret_copies, a1, a2, a3, b1, b2, b3):
        for copy in copies:
            copy.wait_send()
    for store in stores:
        store.wait()


def write_kernel(
    nodes_ref, edges_ref, a_ref, b_ref,
    gnodes_ref, gedges_ref, gew1_ref, geb1_ref, gew2_ref, gnw1_ref, gnb1_ref, gnw2_ref,
    nodes_local, edges_local, a_local, b_local, ew1, eb1, ew2, nw1, nb1, nw2, sem,
):
    width = 128
    copies = []

    def write(source, target):
        copy = pltpu.make_async_copy(source, target, sem.at[len(copies)])
        copy.start()
        copies.append(copy)

    load_a = pltpu.make_async_copy(a_ref, a_local, sem.at[8])
    load_b = pltpu.make_async_copy(b_ref, b_local, sem.at[9])
    load_nodes = pltpu.make_async_copy(nodes_ref, nodes_local, sem.at[10])
    load_edges = pltpu.make_async_copy(edges_ref, edges_local, sem.at[11])
    load_edges.start()
    load_b.start()
    load_a.start()
    load_nodes.start()
    load_edges.wait()
    write(edges_local, gedges_ref)
    load_nodes.wait()
    write(nodes_local, gnodes_ref)
    load_b.wait()
    load_a.wait()
    ew1[...] = b_local[: 3 * width, :].astype(F32)
    write(ew1, gew1_ref)
    nw1[...] = a_local[: 2 * width, :].astype(F32)
    write(nw1, gnw1_ref)
    ew2[...] = b_local[3 * width : 4 * width, :].astype(F32)
    write(ew2, gew2_ref)
    nw2[...] = a_local[2 * width : 3 * width, :].astype(F32)
    write(nw2, gnw2_ref)
    eb1[...] = b_local[4 * width : 4 * width + 16, :].astype(F32)[:1]
    write(eb1, geb1_ref)
    nb1[...] = a_local[3 * width : 3 * width + 16, :].astype(F32)[:1]
    write(nb1, gnb1_ref)
    for copy in copies:
        copy.wait()


def local(groups, domains, *args):
    (
        node_feat, edge_feat, edge_src, edge_dst, halo_send, halo_count, par_send, par_count,
        child_slot, pool_weight, parent_grad, edge_w1, edge_b1, edge_w2, node_w1, node_b1, node_w2,
    ) = args
    own, width = node_feat.shape
    edges = edge_feat.shape[0]
    a_block = round_up(-(-(3 * width + 16) // groups), 16)
    b_block = round_up(-(-(4 * width + 16) // groups), 16)
    vmem = pltpu.VMEM
    scratch = [
        vmem((edges, width), jnp.int32),
        vmem((edges, width), jnp.int32),
        vmem((own, edges), BF16),
        vmem((own, edges), BF16),
        vmem((edges, own), BF16),
        vmem((edges, width), F32),
        vmem((edges, width), F32),
        vmem((edges, width), BF16),
        vmem((edges, width), BF16),
        vmem((edges, width), BF16),
        vmem((edges, width), BF16),
        vmem((domains, SLOT, width), F32),
        vmem((domains, SLOT, width), F32),
        vmem((groups, SLOT, width), F32),
        vmem((groups, SLOT, width), F32),
        vmem((domains, SLOT, width), F32),
        vmem((domains, SLOT, width), F32),
    ]
    for block in (a_block, b_block):
        scratch += [
            vmem((groups * block, width), BF16),
            vmem((groups, block, width), BF16),
            vmem((domains, block, width), BF16),
        ]
    scratch += [
        pltpu.SemaphoreType.DMA((5, groups)),
        pltpu.SemaphoreType.DMA((5, groups)),
        pltpu.SemaphoreType.DMA((4, domains)),
        pltpu.SemaphoreType.DMA((4, domains)),
    ]
    shape = jax.ShapeDtypeStruct
    operands = (
        node_feat, edge_feat, edge_src.reshape(edges // 128, 128), edge_dst.reshape(edges // 128, 128),
        halo_send, halo_count, par_send.T, par_count, child_slot[None, :], pool_weight[None, :],
        parent_grad, edge_w1, edge_b1[None, :], edge_w2, node_w1, node_b1[None, :], node_w2,
    )
    results = (
        shape((own, width), BF16),
        shape((edges, width), BF16),
        shape((groups * a_block, width), BF16),
        shape((groups * b_block, width), BF16),
    )
    buffers = [vmem(array.shape, array.dtype) for array in operands + results]
    results = pl.pallas_call(
        functools.partial(kernel, groups, domains),
        out_shape=results,
        in_specs=[pl.BlockSpec(memory_space=pltpu.HBM)] * ARGS,
        out_specs=(pl.BlockSpec(memory_space=pltpu.HBM),) * 4,
        scratch_shapes=buffers
        + [pltpu.SemaphoreType.DMA((ARGS,)), pltpu.SemaphoreType.DMA((4,))]
        + scratch,
        compiler_params=pltpu.CompilerParams(
            collective_id=0, has_side_effects=True, vmem_limit_bytes=60 * 1024 * 1024
        ),
        name="message_layer_grad",
    )(*operands)
    weights = [(3 * width, width), (1, width), (width, width), (2 * width, width), (1, width), (width, width)]
    outs = pl.pallas_call(
        write_kernel,
        out_shape=(shape((own, width), BF16), shape((edges, width), BF16))
        + tuple(shape(size, F32) for size in weights),
        in_specs=[pl.BlockSpec(memory_space=pltpu.HBM)] * 4,
        out_specs=(pl.BlockSpec(memory_space=pltpu.HBM),) * 8,
        scratch_shapes=buffers[-4:]
        + [vmem(size, F32) for size in weights]
        + [pltpu.SemaphoreType.DMA((12,))],
        compiler_params=pltpu.CompilerParams(vmem_limit_bytes=60 * 1024 * 1024),
        name="write_results",
    )(*results)
    return (
        outs[0], outs[1], outs[2], outs[3].reshape(width), outs[4],
        outs[5], outs[6].reshape(width), outs[7],
    )


def solution(mesh):
    rows, flat = P(("grp", "dom"), None), P(("grp", "dom"))
    in_specs = (
        rows, rows, flat, flat, rows, rows, rows, rows, flat, flat, rows,
        P(), P(), P(), P(), P(), P(),
    )
    out_specs = (rows, rows, P(), P(), P(), P(), P(), P())
    return jax.shard_map(
        functools.partial(local, mesh.shape["grp"], mesh.shape["dom"]),
        mesh=mesh, in_specs=in_specs, out_specs=out_specs, check_vma=False,
    )
```
